128 devices in a mesh: row: 8 (over x_lo, y), col: 16 (over x_hi, z, core).
Axes of the slice: x: 4 (x_hi: 2, x_lo: 2; x = x_hi * 2 + x_lo), y: 4, z: 4, core: 2. Of those that a mesh axis runs over, the one named last changes fastest.
Arguments:
- latent: bfloat16 [8, 64, 64, 640], P(None, 'row', 'col'), may hold values from -6 to 6
- gn1_gain: float32 [640], replicated, may hold values from 0.5 to 1.5
- gn1_bias: float32 [640], replicated, may hold values from -1.75 to 1.75
- conv1_weight: bfloat16 [3, 3, 640, 640], replicated, may hold values from -0.078125 to 0.078125
- conv1_bias: float32 [640], replicated, may hold values from -1.75 to 1.75
- time_shift: float32 [8, 640], replicated, may hold values from -6 to 6
- gn2_gain: float32 [640], replicated, may hold values from 0.5 to 1.5
- gn2_bias: float32 [640], replicated, may hold values from -1.75 to 1.75
- conv2_weight: bfloat16 [3, 3, 640, 640], replicated, may hold values from -0.078125 to 0.078125
- conv2_bias: float32 [640], replicated, may hold values from -1.75 to 1.75
- gn3_gain: float32 [640], replicated, may hold values from 0.5 to 1.5
- gn3_bias: float32 [640], replicated, may hold values from -1.75 to 1.75
- in_weight: bfloat16 [640, 640], replicated, may hold values from -0.25 to 0.25
- in_bias: float32 [640], replicated, may hold values from -1.75 to 1.75
- ln_gain: float32 [640], replicated, may hold values from 0.5 to 1.5
- ln_bias: float32 [640], replicated, may hold values from -1.75 to 1.75
- query_weight: bfloat16 [640, 640], replicated, may hold values from -0.5 to 0.5
- key_weight: bfloat16 [640, 640], replicated, may hold values from -0.5 to 0.5
- value_weight: bfloat16 [640, 640], replicated, may hold values from -0.25 to 0.25
- out_weight: bfloat16 [640, 640], replicated, may hold values from -0.25 to 0.25
- out_bias: float32 [640], replicated, may hold values from -1.75 to 1.75
- proj_weight: bfloat16 [640, 640], replicated, may hold values from -0.25 to 0.25
- proj_bias: float32 [640], replicated, may hold values from -1.75 to 1.75
Outputs:
- block_out: bfloat16 [8, 64, 64, 640], P('row', None, 'col')
The draws below stay inside these ranges and needn't reach their ends.
All inputs are finite; a program needn't handle non-finite values.
Results may differ from the reference program's by a relative error of at most 0.024.
Values may be sent and summed in bfloat16 or wider, within the bound.
A program may use at most 192 MiB of HBM per device.

```python
import math
import jax
import jax.numpy as jnp
from jax import lax

C = 640
HEADS = 10
HEAD_DIM = 64
GROUPS = 32
IMAGES = 8
H = 64
W = 64


def base_matrix(key):
    entries = jax.random.normal(key, (C, C), jnp.float32)
    return jnp.clip(entries, -6.0, 6.0) * C ** (-0.5)


def spatial_scale(low, ratio):
    row_pos = jnp.arange(H, dtype=jnp.float32) / max(H - 1, 1)
    col_pos = jnp.arange(W, dtype=jnp.float32) / max(W - 1, 1)
    ramp = 0.5 * (row_pos[:, None] + col_pos[None, :])
    return low * jnp.exp(ramp * jnp.log(ratio))


def draw_latent(key, part):
    key = jax.random.fold_in(key, 37)
    entries = jnp.clip(jax.random.normal(key, (IMAGES, H, W, C), jnp.float32), -4.0, 4.0)
    scale = spatial_scale(0.25, 6.0)
    return (entries * scale[None, :, :, None]).astype(jnp.bfloat16)


def draw_query_weight(key, part):
    key = jax.random.fold_in(key, 11)
    matrix = base_matrix(jax.random.fold_in(key, 1))
    return jnp.clip(matrix, -0.5, 0.5).astype(jnp.bfloat16)


def draw_key_weight(key, part):
    key = jax.random.fold_in(key, 23)
    matrix = base_matrix(jax.random.fold_in(key, 1))
    return jnp.clip(matrix, -0.5, 0.5).astype(jnp.bfloat16)


def normal_values(key, dims, scale, most, kind=jnp.bfloat16):
    return jnp.clip(scale * jax.random.normal(key, dims, jnp.float32), -most, most).astype(kind)


def setup_inputs(seed: int = 0) -> dict:
    seeds = jax.random.split(jax.random.key(seed), 24)
    latent = draw_latent(jax.random.fold_in(seeds[23], 71), 0)
    gn1_gain = jnp.clip(1.0 + 0.1 * jax.random.normal(seeds[1], (C,), jnp.float32), 0.5, 1.5)
    gn1_bias = normal_values(seeds[2], (C,), 0.3, 1.75, jnp.float32)
    conv1_weight = normal_values(seeds[3], (3, 3, C, C), (9 * C) ** -0.5, 0.078125)
    conv1_bias = normal_values(seeds[4], (C,), 0.3, 1.75, jnp.float32)
    time_shift = normal_values(seeds[5], (IMAGES, C), 1.0, 6.0, jnp.float32)
    gn2_gain = jnp.clip(1.0 + 0.1 * jax.random.normal(seeds[6], (C,), jnp.float32), 0.5, 1.5)
    gn2_bias = normal_values(seeds[7], (C,), 0.3, 1.75, jnp.float32)
    conv2_weight = normal_values(seeds[8], (3, 3, C, C), (9 * C) ** -0.5, 0.078125)
    conv2_bias = normal_values(seeds[9], (C,), 0.3, 1.75, jnp.float32)
    gn3_gain = jnp.clip(1.0 + 0.1 * jax.random.normal(seeds[10], (C,), jnp.float32), 0.5, 1.5)
    gn3_bias = normal_values(seeds[11], (C,), 0.3, 1.75, jnp.float32)
    in_weight = normal_values(seeds[12], (C, C), C ** -0.5, 0.25)
    in_bias = normal_values(seeds[13], (C,), 0.3, 1.75, jnp.float32)
    ln_gain = jnp.clip(1.0 + 0.1 * jax.random.normal(seeds[14], (C,), jnp.float32), 0.5, 1.5)
    ln_bias = normal_values(seeds[15], (C,), 0.3, 1.75, jnp.float32)
    query_weight = draw_query_weight(jax.random.fold_in(seeds[23], 71), 0)
    key_weight = draw_key_weight(jax.random.fold_in(seeds[23], 71), 0)
    value_weight = normal_values(seeds[18], (C, C), C ** -0.5, 0.25)
    out_weight = normal_values(seeds[19], (C, C), C ** -0.5, 0.25)
    out_bias = normal_values(seeds[20], (C,), 0.3, 1.75, jnp.float32)
    proj_weight = normal_values(seeds[21], (C, C), C ** -0.5, 0.25)
    proj_bias = normal_values(seeds[22], (C,), 0.3, 1.75, jnp.float32)
    return dict(latent=latent, gn1_gain=gn1_gain, gn1_bias=gn1_bias, conv1_weight=conv1_weight, conv1_bias=conv1_bias, time_shift=time_shift, gn2_gain=gn2_gain, gn2_bias=gn2_bias, conv2_weight=conv2_weight, conv2_bias=conv2_bias, gn3_gain=gn3_gain, gn3_bias=gn3_bias, in_weight=in_weight, in_bias=in_bias, ln_gain=ln_gain, ln_bias=ln_bias, query_weight=query_weight, key_weight=key_weight, value_weight=value_weight, out_weight=out_weight, out_bias=out_bias, proj_weight=proj_weight, proj_bias=proj_bias)


def moments(values, groups):
    images, height, breadth, channels = values.shape
    grouped = values.reshape(images, height * breadth, groups, channels // groups)
    return (lax.optimization_barrier(jnp.sum(grouped, axis=(1, 3))), lax.optimization_barrier(jnp.sum(grouped * grouped, axis=(1, 3))))

def normalize(values, first_sum, second_sum, cells, gain_vec, bias_vec, epsilon):
    average = first_sum / cells
    variance = second_sum / cells - average * average
    inverse = lax.rsqrt(variance + epsilon)
    group_size = values.shape[-1] // first_sum.shape[-1]
    average_c = jnp.repeat(average, group_size, axis=1)[:, None, None, :]
    inverse_c = jnp.repeat(inverse, group_size, axis=1)[:, None, None, :]
    return (values - average_c) * inverse_c * gain_vec + bias_vec

def group_norm(values, gain_vec, bias_vec, epsilon):
    first_sum, second_sum = moments(values, GROUPS)
    cells = values.shape[1] * values.shape[2] * (values.shape[3] // GROUPS)
    return normalize(values, first_sum, second_sum, cells, gain_vec, bias_vec, epsilon)

def convolve(activation, weight, bias_vec):
    images, height, breadth, channels = activation.shape
    padded = jnp.pad(activation, ((0, 0), (1, 1), (1, 1), (0, 0)))
    summed = jnp.zeros((images * height * breadth, weight.shape[3]), jnp.float32)
    for shift_row in range(3):
        for shift_col in range(3):
            window = padded[:, shift_row:shift_row + height, shift_col:shift_col + breadth, :]
            summed = summed + jnp.dot(window.reshape(-1, channels), weight[shift_row, shift_col], preferred_element_type=jnp.float32)
    return summed.reshape(images, height, breadth, -1) + bias_vec

def layer_norm(values, gain_vec, bias_vec):
    average = lax.optimization_barrier(jnp.mean(values, axis=-1, keepdims=True))
    centered = values - average
    variance = lax.optimization_barrier(jnp.mean(centered * centered, axis=-1, keepdims=True))
    return centered * lax.rsqrt(variance + 1e-05) * gain_vec + bias_vec

def attend_image(operands):
    queries, keys, values = operands
    tokens = queries.shape[0]
    block_rows = math.gcd(tokens, 512)
    key_heads = keys.astype(jnp.float32).reshape(tokens, HEADS, HEAD_DIM)
    value_heads = values.astype(jnp.float32).reshape(tokens, HEADS, HEAD_DIM)

    def one_block(query_block):
        query_heads = query_block.astype(jnp.float32).reshape(block_rows, HEADS, HEAD_DIM)
        scores = jnp.einsum('qhd,khd->hqk', query_heads, key_heads) * HEAD_DIM ** (-0.5)
        highest = lax.optimization_barrier(jnp.max(scores, axis=-1, keepdims=True))
        expo = jnp.exp(scores - highest)
        summed = lax.optimization_barrier(jnp.sum(expo, axis=-1))
        rounded = lax.optimization_barrier(expo.astype(jnp.bfloat16)).astype(jnp.float32)
        weighted = jnp.einsum('hqk,khd->qhd', rounded, value_heads)
        weighted = weighted / summed.T[:, :, None]
        return weighted.reshape(block_rows, HEADS * HEAD_DIM).astype(jnp.bfloat16)
    blocks = lax.map(one_block, queries.reshape(tokens // block_rows, block_rows, -1))
    return blocks.reshape(tokens, -1)

def reference(latent, gn1_gain, gn1_bias, conv1_weight, conv1_bias, time_shift, gn2_gain, gn2_bias, conv2_weight, conv2_bias, gn3_gain, gn3_bias, in_weight, in_bias, ln_gain, ln_bias, query_weight, key_weight, value_weight, out_weight, out_bias, proj_weight, proj_bias):
    source = latent.astype(jnp.float32)
    first_act = jax.nn.silu(group_norm(source, gn1_gain, gn1_bias, 1e-05)).astype(jnp.bfloat16)
    first_conv = convolve(first_act, conv1_weight, conv1_bias) + time_shift[:, None, None, :]
    second_act = jax.nn.silu(group_norm(first_conv, gn2_gain, gn2_bias, 1e-05)).astype(jnp.bfloat16)
    resnet_out = (source + convolve(second_act, conv2_weight, conv2_bias)).astype(jnp.bfloat16)
    resnet_f32 = resnet_out.astype(jnp.float32)
    attn_in = group_norm(resnet_f32, gn3_gain, gn3_bias, 1e-06).astype(jnp.bfloat16)
    channels = latent.shape[3]
    flat = attn_in.reshape(-1, channels)
    inner = (jnp.dot(flat, in_weight, preferred_element_type=jnp.float32) + in_bias).astype(jnp.bfloat16)
    normed = layer_norm(inner.astype(jnp.float32), ln_gain, ln_bias).astype(jnp.bfloat16)
    queries = jnp.dot(normed, query_weight, preferred_element_type=jnp.float32).astype(jnp.bfloat16)
    keys = jnp.dot(normed, key_weight, preferred_element_type=jnp.float32).astype(jnp.bfloat16)
    values = jnp.dot(normed, value_weight, preferred_element_type=jnp.float32).astype(jnp.bfloat16)
    images = latent.shape[0]
    per_image = H * W
    attended = lax.map(attend_image, (queries.reshape(images, per_image, channels), keys.reshape(images, per_image, channels), values.reshape(images, per_image, channels)))
    attended = attended.reshape(-1, channels)
    mixed = (inner.astype(jnp.float32) + jnp.dot(attended, out_weight, preferred_element_type=jnp.float32) + out_bias).astype(jnp.bfloat16)
    projected = jnp.dot(mixed, proj_weight, preferred_element_type=jnp.float32) + proj_bias
    return (resnet_f32 + projected.reshape(resnet_out.shape)).astype(jnp.bfloat16)
```

```python
import jax
import jax.numpy as jnp
from jax import lax
from jax.experimental import pallas as pl
from jax.experimental.pallas import tpu as pltpu
from jax.sharding import PartitionSpec as P

MESH = pl.DeviceIdType.MESH
F32 = jnp.float32
BF16 = jnp.bfloat16
C = 640
ROWS = 64
OWN = 4
CELLS = 64 * 64 * 20
LANES = 128
UNITS = 10
ORDER = [(0, 0), (0, 1), (1, 0), (0, 3), (1, 1), (0, 2), (1, 3), (1, 2)]
STAGES = [
    [("own", 0), ("own", 1)],
    [("own", 2), ("own", 3), ("sib", 0), ("sib", 1)],
    [("own", 4), ("own", 5), ("sib", 2), ("sib", 3)],
    [("own", 6), ("own", 7), ("sib", 4), ("sib", 5)],
    [("sib", 6), ("sib", 7)],
]


def dot(a, b):
    return jnp.dot(a, b, preferred_element_type=F32)


def kernel(
    lat, conv1_w, conv2_w, in_w, q_w, k_w, v_w, out_w, proj_w,
    gn1_g, gn1_b, conv1_b, tshift, gn2_g, gn2_b, conv2_b, gn3_g, gn3_b,
    in_b, ln_g, ln_b, out_b, proj_b,
    result,
    w1, w2, wd, group, xin, xcol, stats, parts, taps, conv, resnet, inner,
    qpack, kv, qbuf, queries, kvbuf, vstage, accum, highest, opack, back,
    wsem, a2a_s, a2a_r, halo_s, halo_r, st_s, st_r, q_s, q_r, kv_s, kv_r, fw_s, fw_r, o_s, o_r,
):
    row = lax.axis_index("row")
    col = lax.axis_index("col")
    plane, z, core = lax.div(col, 8), lax.rem(lax.div(col, 2), 4), lax.rem(col, 2)

    def remote(src, dst, send, recv, where):
        return pltpu.make_async_remote_copy(
            src_ref=src, dst_ref=dst, send_sem=send, recv_sem=recv,
            device_id=where, device_id_type=MESH,
        )

    loads = []

    def load(src, dst):
        copy = pltpu.make_async_copy(src, dst, wsem.at[len(loads)])
        copy.start()
        loads.append(copy)

    for source, target in ((conv1_w, w1), (conv2_w, w2)):
        for dx in range(3):
            for dy in range(3):
                load(source.at[dy, dx], target.at[dx, pl.ds(dy * C, C)])
    for i, source in enumerate((in_w, q_w, k_w, v_w, out_w, proj_w)):
        load(source, wd.at[i])

    barrier = pltpu.get_barrier_semaphore()
    for t in range(1, 8):
        pl.semaphore_signal(
            barrier, inc=1, device_id=(lax.rem(row + t, 8), col), device_id_type=MESH
        )
    for t in range(1, 16):
        pl.semaphore_signal(
            barrier, inc=1, device_id=(row, lax.rem(col + t, 16)), device_id_type=MESH
        )
    one = lax.shift_right_logical(lax.broadcasted_iota(jnp.int32, (C, C), 0) * 52429, 20)
    two = lax.shift_right_logical(lax.broadcasted_iota(jnp.int32, (C, C), 1) * 52429, 20)
    group[...] = jnp.where(one == two, 1.0, 0.0).astype(BF16)
    parts[...] = jnp.zeros_like(parts)
    xin[pl.ds(row, 1)] = lat[pl.ds(row, 1)]
    pl.semaphore_wait(barrier, 22)

    swaps = []
    for t in range(1, 8):
        to, frm = lax.rem(row + t, 8), lax.rem(row + 8 - t, 8)
        copy = remote(lat.at[to], xin.at[row], a2a_s.at[t], a2a_r.at[t], (to, col))
        copy.start()
        swaps.append(copy)
    arrived = [
        remote(lat.at[0], xin.at[lax.rem(row + 8 - t, 8)], a2a_s.at[t], a2a_r.at[t], (lax.rem(row + t, 8), col))
        for t in range(1, 8)
    ]
    for copy in arrived:
        copy.wait_recv()
    first = jnp.zeros((8, C), F32)
    second = jnp.zeros((8, C), F32)
    for i in range(4):
        upper = xin[2 * i].astype(F32)
        lower = xin[2 * i + 1].astype(F32)
        for j in range(OWN):
            a, b = upper[8 * j : 8 * j + 8], lower[8 * j : 8 * j + 8]
            first = first + a + b
            second = second + a * a + b * b
            xcol[2 + j, 16 * i : 16 * i + 16, :] = jnp.concatenate([a, b], axis=0).astype(BF16)

    right, left = lax.rem(col + 1, 16), lax.rem(col + 15, 16)
    halos = [
        remote(xcol.at[pl.ds(4, 2)], xcol.at[pl.ds(0, 2)], halo_s.at[0], halo_r.at[0], (row, right)),
        remote(xcol.at[pl.ds(2, 2)], xcol.at[pl.ds(6, 2)], halo_s.at[1], halo_r.at[1], (row, left)),
    ]
    sums = []

    def send_sums(phase, first, second):
        stats[phase, pl.ds(col, 1)] = jnp.concatenate(
            [jnp.sum(first, axis=0, keepdims=True), jnp.sum(second, axis=0, keepdims=True)], axis=0
        )[None]
        for t in range(1, 16):
            copy = remote(
                stats.at[phase, col], stats.at[phase, col], st_s.at[phase, t], st_r.at[phase, t],
                (row, lax.rem(col + t, 16)),
            )
            copy.start()
            sums.append(copy)

    def take_sums(phase, gain, bias, epsilon):
        for t in range(1, 16):
            remote(
                stats.at[phase, col], stats.at[phase, lax.rem(col + 16 - t, 16)],
                st_s.at[phase, t], st_r.at[phase, t], (row, lax.rem(col + t, 16)),
            ).wait_recv()
        total = jnp.sum(stats[phase], axis=0)
        high = total.astype(BF16).astype(F32)
        rest = total - high
        middle = rest.astype(BF16).astype(F32)
        parts[0:2] = high
        parts[2:4] = middle
        parts[4:6] = rest - middle
        spread = dot(parts[...].astype(BF16), group[...])
        mean = (spread[0:1] + spread[2:3] + spread[4:5]) * (1.0 / CELLS)
        square = (spread[1:2] + spread[3:4] + spread[5:6]) * (1.0 / CELLS)
        scale = lax.rsqrt(square - mean * mean + epsilon) * gain[...]
        return scale, bias[...] - mean * scale

    def put_taps(place, values, scale, shift, column):
        v = values * scale + shift
        act = 0.5 * v * (1.0 + jnp.tanh(0.5 * v))
        act = jnp.where((column >= 0) & (column < 64), act, 0.0)
        index = lax.broadcasted_iota(jnp.int32, (ROWS, C), 0)
        above = jnp.where(index == 0, 0.0, pltpu.roll(act, 1, 0))
        below = jnp.where(index == ROWS - 1, 0.0, pltpu.roll(act, ROWS - 1, 0))
        taps[pl.ds(place, 1), :, 0:C] = above.astype(BF16)[None]
        taps[pl.ds(place, 1), :, C : 2 * C] = act.astype(BF16)[None]
        taps[pl.ds(place, 1), :, 2 * C : 3 * C] = below.astype(BF16)[None]

    for copy in halos:
        copy.start()
    send_sums(0, first, second)
    scale1, shift1 = take_sums(0, gn1_g, gn1_b, 1e-5)
    for copy in halos:
        copy.wait_recv()

    @pl.loop(0, 8)
    def _(j):
        values = xcol[pl.ds(j, 1)].reshape(ROWS, C).astype(F32)
        put_taps(j, values, scale1, shift1, 4 * col - 2 + j)

    for copy in loads[:9]:
        copy.wait()
    conv[...] = jnp.broadcast_to(conv1_b[...] + tshift[pl.ds(row, 1), :], conv.shape)

    @pl.loop(0, 3)
    def _(dx):
        lhs = taps[pl.ds(dx, 6)].reshape(6 * ROWS, 3 * C)
        conv[...] += dot(lhs, w1[pl.ds(dx, 1)].reshape(3 * C, C))

    own = conv[ROWS : 5 * ROWS, :].reshape(32, 8, C)
    send_sums(1, jnp.sum(own, axis=0), jnp.sum(own * own, axis=0))
    scale2, shift2 = take_sums(1, gn2_g, gn2_b, 1e-5)

    @pl.loop(0, 6)
    def _(j):
        values = conv[pl.ds(pl.multiple_of(j * ROWS, ROWS), ROWS), :]
        put_taps(j, values, scale2, shift2, 4 * col - 1 + j)

    for copy in loads[9:18]:
        copy.wait()
    conv[0 : 4 * ROWS, :] = xcol[2:6].reshape(4 * ROWS, C).astype(F32) + conv2_b[...]

    @pl.loop(0, 3)
    def _(dx):
        lhs = taps[pl.ds(dx, 4)].reshape(4 * ROWS, 3 * C)
        conv[0 : 4 * ROWS, :] += dot(lhs, w2[pl.ds(dx, 1)].reshape(3 * C, C))

    resnet[...] = conv[0 : 4 * ROWS, :].astype(BF16)
    rounded = resnet[...].astype(F32).reshape(32, 8, C)
    send_sums(2, jnp.sum(rounded, axis=0), jnp.sum(rounded * rounded, axis=0))
    for copy in loads[18:]:
        copy.wait()
    scale3, shift3 = take_sums(2, gn3_g, gn3_b, 1e-6)

    attn_in = (resnet[...].astype(F32) * scale3 + shift3).astype(BF16)
    inner[...] = (dot(attn_in, wd[0]) + in_b[...]).astype(BF16)
    v = inner[...].astype(F32)
    centered = v - jnp.mean(v, axis=-1, keepdims=True)
    variance = jnp.mean(centered * centered, axis=-1, keepdims=True)
    normed = (centered * lax.rsqrt(variance + 1e-5) * ln_g[...] + ln_b[...]).astype(BF16)

    half = lax.broadcasted_iota(jnp.int32, (128, LANES), 1) < 64
    half2 = lax.broadcasted_iota(jnp.int32, (256, LANES), 1) < 64

    def swap(a):
        return pltpu.roll(a, 64, 1)

    q = dot(normed, wd[1]).astype(BF16).astype(F32) * 0.125
    for i in range(5):
        a, b = q[0:128, i * LANES : (i + 1) * LANES], q[128:256, i * LANES : (i + 1) * LANES]
        qpack[2 * i] = jnp.where(half, a, swap(b)).astype(BF16)
        qpack[2 * i + 1] = jnp.where(half, swap(a), b).astype(BF16)

    def place_of(head):
        unit = 16 * (head % 5) + col
        return (head // 5) * 8 + lax.div(unit, 20) * 2 + core, lax.div(lax.rem(unit, 20), 2)

    for head in range(10):
        to, slot = place_of(head)
        copy = remote(qpack.at[head], qbuf.at[slot], q_s.at[head], q_r.at[slot], (row, to))

        @pl.when(to != col)
        def _():
            copy.start()

        @pl.when(to == col)
        def _():
            qbuf[pl.ds(slot, 1)] = qpack[head][None]

    keys = dot(normed, wd[2])
    values = dot(normed, wd[3])
    for i in range(5):
        a, b = keys[:, i * LANES : (i + 1) * LANES], values[:, i * LANES : (i + 1) * LANES]
        kv[2 * i] = jnp.where(half2, a, swap(b)).astype(BF16)
        kv[2 * i + 1] = jnp.where(half2, swap(a), b).astype(BF16)

    def chip(dx, dz):
        return lax.rem(plane + dx, 2), lax.rem(z + dz, 4)

    here = plane * 4 + z
    kvbuf[pl.ds(core, 1), pl.ds(here, 1)] = kv[pl.ds(5 * plane + z, 2)][None, None]
    spreads = []
    for t, (dx, dz) in enumerate(ORDER):
        if t == 0:
            continue
        p2, z2 = chip(dx, dz)
        copy = remote(
            kv.at[pl.ds(5 * p2 + z2, 2)], kvbuf.at[core, here], kv_s.at[t], kv_r.at[t],
            (row, p2 * 8 + z2 * 2 + core),
        )
        copy.start()
        spreads.append(copy)

    sibling = (row, plane * 8 + z * 2 + 1 - core)

    def source(t):
        dx, dz = ORDER[t]
        p2, z2 = chip(dx, 4 - dz)
        return p2 * 4 + z2

    def unit_of(j):
        unit = 20 * z + 2 * j + core
        head, block = lax.div(unit, 16), lax.rem(unit, 16)
        return head, block

    for j in range(UNITS):
        head, block = unit_of(j)

        @pl.when(block != col)
        def _():
            remote(qpack.at[0], qbuf.at[j], q_s.at[0], q_r.at[j], (row, block)).wait_recv()

    @pl.loop(0, UNITS)
    def _(j):
        packed = qbuf[pl.ds(j, 1)].reshape(128, LANES).astype(F32)
        low = jnp.where(half, packed, 0.0).astype(BF16)
        high = jnp.where(half, swap(packed), 0.0).astype(BF16)
        queries[pl.ds(j, 1)] = jnp.concatenate([low, high], axis=0)[None]

    lane = lax.broadcasted_iota(jnp.int32, (1, LANES), 1)
    keep = jnp.where(lane < 64, 0.0, 1.0).astype(BF16)
    ones = jnp.where(lane < 64, 1.0, 0.0).astype(BF16)
    forwards, returns = [], []
    for number, blocks in enumerate(STAGES):
        start, end = number == 0, number == len(STAGES) - 1
        width = 256 * len(blocks)
        slots = []
        for kind, t in blocks:
            g = source(t)
            if kind == "own":
                if t:
                    remote(
                        kv.at[pl.ds(0, 2)], kvbuf.at[core, g], kv_s.at[t], kv_r.at[t], sibling
                    ).wait_recv()
                copy = remote(kvbuf.at[core, g], kvbuf.at[core, g], fw_s.at[t], fw_r.at[t], sibling)
                copy.start()
                forwards.append(copy)
                slots.append((core, g))
        for kind, t in blocks:
            g = source(t)
            if kind == "sib":
                remote(
                    kvbuf.at[core, g], kvbuf.at[1 - core, g], fw_s.at[t], fw_r.at[t], sibling
                ).wait_recv()
                slots.append((1 - core, g))
        for head in range(2):
            for i, (parity, g) in enumerate(slots):
                block = kvbuf[pl.ds(parity, 1), pl.ds(g, 1), head].reshape(256, LANES)
                vstage[0, head, 256 * i : 256 * i + 256, :] = block
                vstage[1, head, 256 * i : 256 * i + 256, :] = block * keep + ones

        @pl.loop(0, UNITS)
        def _(j):
            head, block = unit_of(j)
            slot = head - z
            packed = []
            for part in range(2):
                rows = pl.ds(128 * part, 128)
                q = queries[pl.ds(j, 1), rows].reshape(128, LANES)
                k = vstage[0, pl.ds(slot, 1), 0:width].reshape(width, LANES)
                v = vstage[1, pl.ds(slot, 1), 0:width].reshape(width, LANES)
                scores = lax.dot_general(
                    q, k, (((1,), (1,)), ((), ())), preferred_element_type=F32
                )
                most = jnp.broadcast_to(jnp.max(scores, axis=1, keepdims=True), (128, LANES))
                if not start:
                    before = highest[pl.ds(j, 1), rows].reshape(128, LANES)
                    most = jnp.maximum(most, before)
                expo = jnp.exp(scores - jnp.concatenate([most] * (width // LANES), axis=1))
                total = dot(expo.astype(BF16), v)
                if not start:
                    total += accum[pl.ds(j, 1), rows].reshape(128, LANES) * jnp.exp(before - most)
                if end:
                    packed.append(total / swap(total))
                else:
                    highest[pl.ds(j, 1), rows] = most[None]
                    accum[pl.ds(j, 1), rows] = total[None]
            if end:
                opack[pl.ds(j, 1)] = jnp.where(half, swap(packed[0]), packed[1]).astype(BF16)[None]
                whole = 5 * plane + head

                @pl.when(block != col)
                def _():
                    remote(
                        opack.at[j], back.at[whole], o_s.at[j], o_r.at[whole], (row, block)
                    ).start()

                @pl.when(block == col)
                def _():
                    back[pl.ds(whole, 1)] = opack[pl.ds(j, 1)]

    for head in range(10):
        frm, slot = place_of(head)

        @pl.when(frm != col)
        def _():
            remote(opack.at[0], back.at[head], o_s.at[0], o_r.at[head], (row, frm)).wait_recv()

    tiles = []
    for i in range(5):
        a, b = back[2 * i].astype(F32), back[2 * i + 1].astype(F32)
        tiles.append(
            jnp.concatenate([jnp.where(half, a, swap(b)), jnp.where(half, swap(a), b)], axis=0)
        )
    attended = jnp.concatenate(tiles, axis=1).astype(BF16)
    mixed = (inner[...].astype(F32) + dot(attended, wd[4]) + out_b[...]).astype(BF16)
    result[...] = (resnet[...].astype(F32) + dot(mixed, wd[5]) + proj_b[...]).astype(BF16)

    for copy in swaps + halos + sums + spreads + forwards:
        copy.wait_send()
    for head in range(10):
        to, slot = place_of(head)

        @pl.when(to != col)
        def _():
            remote(qpack.at[head], qbuf.at[slot], q_s.at[head], q_r.at[slot], (row, to)).wait_send()

    for j in range(UNITS):
        head, block = unit_of(j)

        @pl.when(block != col)
        def _():
            remote(opack.at[j], back.at[0], o_s.at[j], o_r.at[0], (row, block)).wait_send()


def shards(
    latent, gn1_gain, gn1_bias, conv1_weight, conv1_bias, time_shift, gn2_gain, gn2_bias,
    conv2_weight, conv2_bias, gn3_gain, gn3_bias, in_weight, in_bias, ln_gain, ln_bias,
    query_weight, key_weight, value_weight, out_weight, out_bias, proj_weight, proj_bias,
):
    lat = latent.transpose(0, 2, 1, 3).reshape(8, 32, C)
    vec = lambda a: a.reshape(1, C)
    hbm = pl.BlockSpec(memory_space=pl.ANY)
    vmem = pl.BlockSpec(memory_space=pltpu.VMEM)
    dma = pltpu.SemaphoreType.DMA
    result = pl.pallas_call(
        kernel,
        out_shape=jax.ShapeDtypeStruct((OWN * ROWS, C), BF16),
        in_specs=[vmem] + [hbm] * 8 + [vmem] * 14,
        out_specs=vmem,
        scratch_shapes=[
            pltpu.VMEM((3, 3 * C, C), BF16),
            pltpu.VMEM((3, 3 * C, C), BF16),
            pltpu.VMEM((6, C, C), BF16),
            pltpu.VMEM((C, C), BF16),
            pltpu.VMEM((8, 32, C), BF16),
            pltpu.VMEM((8, ROWS, C), BF16),
            pltpu.VMEM((3, 16, 2, C), F32),
            pltpu.VMEM((8, C), F32),
            pltpu.VMEM((8, ROWS, 3 * C), BF16),
            pltpu.VMEM((6 * ROWS, C), F32),
            pltpu.VMEM((256, C), BF16),
            pltpu.VMEM((256, C), BF16),
            pltpu.VMEM((10, 128, LANES), BF16),
            pltpu.VMEM((10, 256, LANES), BF16),
            pltpu.VMEM((UNITS, 128, LANES), BF16),
            pltpu.VMEM((UNITS, 256, LANES), BF16),
            pltpu.VMEM((2, 8, 2, 256, LANES), BF16),
            pltpu.VMEM((2, 2, 1024, LANES), BF16),
            pltpu.VMEM((UNITS, 256, LANES), F32),
            pltpu.VMEM((UNITS, 256, LANES), F32),
            pltpu.VMEM((UNITS, 128, LANES), BF16),
            pltpu.VMEM((10, 128, LANES), BF16),
            dma((24,)), dma((8,)), dma((8,)), dma((2,)), dma((2,)), dma((3, 16)), dma((3, 16)),
            dma((10,)), dma((10,)), dma((8,)), dma((8,)), dma((8,)), dma((8,)),
            dma((10,)), dma((10,)),
        ],
        compiler_params=pltpu.CompilerParams(
            collective_id=0, has_side_effects=True, vmem_limit_bytes=56 * 2**20
        ),
        cost_estimate=pl.CostEstimate(
            flops=8 * 10**9, bytes_accessed=21 * 10**6, transcendentals=11 * 10**6
        ),
    )(
        lat, conv1_weight, conv2_weight, in_weight, query_weight, key_weight, value_weight,
        out_weight, proj_weight, vec(gn1_gain), vec(gn1_bias), vec(conv1_bias), time_shift,
        vec(gn2_gain), vec(gn2_bias), vec(conv2_bias), vec(gn3_gain), vec(gn3_bias),
        vec(in_bias), vec(ln_gain), vec(ln_bias), vec(out_bias), vec(proj_bias),
    )
    return result.reshape(OWN, ROWS, C).transpose(1, 0, 2)[None]


def solution(mesh):
    placed = (P(None, "row", "col", None),) + (P(),) * 22
    return jax.shard_map(
        shards, mesh=mesh, in_specs=placed, out_specs=P("row", None, "col", None), check_vma=False
    )
```

```python
import jax
import jax.numpy as jnp
from jax import lax
from jax.experimental import pallas as pl
from jax.experimental.pallas import tpu as pltpu
from jax.sharding import PartitionSpec as P

MESH = pl.DeviceIdType.MESH
F32 = jnp.float32
BF16 = jnp.bfloat16
C = 640
ROWS = 64
OWN = 4
CELLS = 64 * 64 * 20
LANES = 128
UNITS = 10
ORDER = [(0, 0), (0, 1), (1, 0), (0, 3), (1, 1), (0, 2), (1, 3), (1, 2)]
STAGES = [
    [(kind, t) for kind in ("own", "sib") for t in range(2 * number, 2 * number + 2)]
    for number in range(4)
]


def dot(a, b):
    return jnp.dot(a, b, preferred_element_type=F32)


def kernel(
    lat, conv1_w, conv2_w, in_w, q_w, k_w, v_w, out_w, proj_w,
    gn1_g, gn1_b, conv1_b, tshift, gn2_g, gn2_b, conv2_b, gn3_g, gn3_b,
    in_b, ln_g, ln_b, out_b, proj_b,
    result,
    w1, w2, wd, group, xin, xcol, stats, parts, taps, conv, resnet, inner,
    qpack, kv, qbuf, queries, kvbuf, vstage, accum, highest, opack, back,
    wsem, a2a_s, a2a_r, halo_s, halo_r, st_s, st_r, q_s, q_r, kv_s, kv_r, fw_s, fw_r, o_s, o_r,
):
    row = lax.axis_index("row")
    col = lax.axis_index("col")
    plane, z, core = lax.div(col, 8), lax.rem(lax.div(col, 2), 4), lax.rem(col, 2)

    def remote(src, dst, send, recv, where):
        return pltpu.make_async_remote_copy(
            src_ref=src, dst_ref=dst, send_sem=send, recv_sem=recv,
            device_id=where, device_id_type=MESH,
        )

    leaving = []

    def send(copy, when=None):
        def start():
            copy.start()

        def leave():
            copy.wait_send()

        if when is None:
            start()
            leaving.append(leave)
        else:
            pl.when(when)(start)
            leaving.append(lambda: pl.when(when)(leave))

    loads = []

    def load(src, dst):
        copy = pltpu.make_async_copy(src, dst, wsem.at[next(used)])
        copy.start()
        loads.append(copy)

    def loaded(count):
        for copy in loads[:count]:
            copy.wait()
        del loads[:count]

    used = iter(range(24))

    for source, target in ((conv1_w, w1), (conv2_w, w2)):
        for dx in range(3):
            for dy in range(3):
                load(source.at[dy, dx], target.at[dx, pl.ds(dy * C, C)])
    for i, source in enumerate((in_w, q_w, k_w, v_w, out_w, proj_w)):
        load(source, wd.at[i])

    barrier = pltpu.get_barrier_semaphore()
    for t in range(1, 8):
        pl.semaphore_signal(
            barrier, inc=1, device_id=(lax.rem(row + t, 8), col), device_id_type=MESH
        )
    for t in range(1, 16):
        pl.semaphore_signal(
            barrier, inc=1, device_id=(row, lax.rem(col + t, 16)), device_id_type=MESH
        )
    one = lax.shift_right_logical(lax.broadcasted_iota(jnp.int32, (C, C), 0) * 52429, 20)
    two = lax.shift_right_logical(lax.broadcasted_iota(jnp.int32, (C, C), 1) * 52429, 20)
    group[...] = jnp.where(one == two, 1.0, 0.0).astype(BF16)
    parts[...] = jnp.zeros_like(parts)
    xin[pl.ds(row, 1)] = lat[pl.ds(row, 1)]
    pl.semaphore_wait(barrier, 22)

    for t in range(1, 8):
        to = lax.rem(row + t, 8)
        send(remote(lat.at[to], xin.at[row], a2a_s.at[t], a2a_r.at[t], (to, col)))
    arrived = [
        remote(lat.at[0], xin.at[lax.rem(row + 8 - t, 8)], a2a_s.at[t], a2a_r.at[t], (lax.rem(row + t, 8), col))
        for t in range(1, 8)
    ]
    for copy in arrived:
        copy.wait_recv()
    first = jnp.zeros((8, C), F32)
    second = jnp.zeros((8, C), F32)
    for i in range(4):
        upper = xin[2 * i].astype(F32)
        lower = xin[2 * i + 1].astype(F32)
        for j in range(OWN):
            a, b = upper[8 * j : 8 * j + 8], lower[8 * j : 8 * j + 8]
            first = first + a + b
            second = second + a * a + b * b
            xcol[2 + j, 16 * i : 16 * i + 16, :] = jnp.concatenate([a, b], axis=0).astype(BF16)

    right, left = lax.rem(col + 1, 16), lax.rem(col + 15, 16)
    halos = [
        remote(xcol.at[pl.ds(4, 2)], xcol.at[pl.ds(0, 2)], halo_s.at[0], halo_r.at[0], (row, right)),
        remote(xcol.at[pl.ds(2, 2)], xcol.at[pl.ds(6, 2)], halo_s.at[1], halo_r.at[1], (row, left)),
    ]
    def send_sums(phase, first, second):
        stats[phase, pl.ds(col, 1)] = jnp.concatenate(
            [jnp.sum(first, axis=0, keepdims=True), jnp.sum(second, axis=0, keepdims=True)], axis=0
        )[None]
        for t in range(1, 16):
            send(remote(
                stats.at[phase, col], stats.at[phase, col], st_s.at[phase, t], st_r.at[phase, t],
                (row, lax.rem(col + t, 16)),
            ))

    def take_sums(phase, gain, bias, epsilon):
        for t in range(1, 16):
            remote(
                stats.at[phase, col], stats.at[phase, lax.rem(col + 16 - t, 16)],
                st_s.at[phase, t], st_r.at[phase, t], (row, lax.rem(col + t, 16)),
            ).wait_recv()
        total = jnp.sum(stats[phase], axis=0)
        high = total.astype(BF16).astype(F32)
        rest = total - high
        middle = rest.astype(BF16).astype(F32)
        parts[0:2] = high
        parts[2:4] = middle
        parts[4:6] = rest - middle
        spread = dot(parts[...].astype(BF16), group[...])
        mean = (spread[0:1] + spread[2:3] + spread[4:5]) * (1.0 / CELLS)
        square = (spread[1:2] + spread[3:4] + spread[5:6]) * (1.0 / CELLS)
        scale = lax.rsqrt(square - mean * mean + epsilon) * gain[...].reshape(1, C)
        return scale, bias[...].reshape(1, C) - mean * scale

    def put_taps(place, values, scale, shift, column):
        v = values * scale + shift
        act = 0.5 * v * (1.0 + jnp.tanh(0.5 * v))
        act = jnp.where((column >= 0) & (column < 64), act, 0.0)
        index = lax.broadcasted_iota(jnp.int32, (ROWS, C), 0)
        above = jnp.where(index == 0, 0.0, pltpu.roll(act, 1, 0))
        below = jnp.where(index == ROWS - 1, 0.0, pltpu.roll(act, ROWS - 1, 0))
        taps[pl.ds(place, 1), :, 0:C] = above.astype(BF16)[None]
        taps[pl.ds(place, 1), :, C : 2 * C] = act.astype(BF16)[None]
        taps[pl.ds(place, 1), :, 2 * C : 3 * C] = below.astype(BF16)[None]

    for copy in halos:
        send(copy)
    send_sums(0, first, second)
    scale1, shift1 = take_sums(0, gn1_g, gn1_b, 1e-5)
    for copy in halos:
        copy.wait_recv()

    @pl.loop(0, 8)
    def _(j):
        values = xcol[pl.ds(j, 1)].reshape(ROWS, C).astype(F32)
        put_taps(j, values, scale1, shift1, 4 * col - 2 + j)

    loaded(9)
    conv[...] = jnp.broadcast_to(conv1_b[...].reshape(1, C) + tshift[pl.ds(row, 1), :], conv.shape)

    @pl.loop(0, 3)
    def _(dx):
        lhs = taps[pl.ds(dx, 6)].reshape(6 * ROWS, 3 * C)
        conv[...] += dot(lhs, w1[pl.ds(dx, 1)].reshape(3 * C, C))

    own = conv[ROWS : 5 * ROWS, :].reshape(32, 8, C)
    send_sums(1, jnp.sum(own, axis=0), jnp.sum(own * own, axis=0))
    scale2, shift2 = take_sums(1, gn2_g, gn2_b, 1e-5)

    @pl.loop(0, 6)
    def _(j):
        values = conv[pl.ds(pl.multiple_of(j * ROWS, ROWS), ROWS), :]
        put_taps(j, values, scale2, shift2, 4 * col - 1 + j)

    loaded(9)
    conv[0 : 4 * ROWS, :] = xcol[2:6].reshape(4 * ROWS, C).astype(F32) + conv2_b[...].reshape(1, C)

    @pl.loop(0, 3)
    def _(dx):
        lhs = taps[pl.ds(dx, 4)].reshape(4 * ROWS, 3 * C)
        conv[0 : 4 * ROWS, :] += dot(lhs, w2[pl.ds(dx, 1)].reshape(3 * C, C))

    resnet[...] = conv[0 : 4 * ROWS, :].astype(BF16)
    rounded = resnet[...].astype(F32).reshape(32, 8, C)
    send_sums(2, jnp.sum(rounded, axis=0), jnp.sum(rounded * rounded, axis=0))
    loaded(6)
    scale3, shift3 = take_sums(2, gn3_g, gn3_b, 1e-6)

    attn_in = (resnet[...].astype(F32) * scale3 + shift3).astype(BF16)
    inner[...] = (dot(attn_in, wd[0]) + in_b[...].reshape(1, C)).astype(BF16)
    v = inner[...].astype(F32)
    centered = v - jnp.mean(v, axis=-1, keepdims=True)
    variance = jnp.mean(centered * centered, axis=-1, keepdims=True)
    normed = (centered * lax.rsqrt(variance + 1e-5) * ln_g[...].reshape(1, C) + ln_b[...].reshape(1, C)).astype(BF16)

    half = lax.broadcasted_iota(jnp.int32, (128, LANES), 1) < 64
    half2 = lax.broadcasted_iota(jnp.int32, (256, LANES), 1) < 64

    def swap(a):
        return pltpu.roll(a, 64, 1)

    q = dot(normed, wd[1]).astype(BF16).astype(F32) * 0.125
    for i in range(5):
        a, b = q[0:128, i * LANES : (i + 1) * LANES], q[128:256, i * LANES : (i + 1) * LANES]
        qpack[2 * i] = jnp.where(half, a, swap(b)).astype(BF16)
        qpack[2 * i + 1] = jnp.where(half, swap(a), b).astype(BF16)

    def place_of(head):
        unit = 16 * (head % 5) + col
        return (head // 5) * 8 + lax.div(unit, 20) * 2 + core, lax.div(lax.rem(unit, 20), 2)

    for head in range(10):
        to, slot = place_of(head)
        send(remote(qpack.at[head], qbuf.at[slot], q_s.at[head], q_r.at[slot], (row, to)), to != col)

        @pl.when(to == col)
        def _():
            qbuf[pl.ds(slot, 1)] = qpack[head][None]

    keys = dot(normed, wd[2])
    values = dot(normed, wd[3])
    for i in range(5):
        a, b = keys[:, i * LANES : (i + 1) * LANES], values[:, i * LANES : (i + 1) * LANES]
        kv[2 * i] = jnp.where(half2, a, swap(b)).astype(BF16)
        kv[2 * i + 1] = jnp.where(half2, swap(a), b).astype(BF16)

    def chip(dx, dz):
        return lax.rem(plane + dx, 2), lax.rem(z + dz, 4)

    here = plane * 4 + z
    kvbuf[pl.ds(core, 1), pl.ds(here, 1)] = kv[pl.ds(5 * plane + z, 2)][None, None]
    for t, (dx, dz) in enumerate(ORDER):
        if t == 0:
            continue
        p2, z2 = chip(dx, dz)
        send(remote(
            kv.at[pl.ds(5 * p2 + z2, 2)], kvbuf.at[core, here], kv_s.at[t], kv_r.at[t],
            (row, p2 * 8 + z2 * 2 + core),
        ))

    sibling = (row, plane * 8 + z * 2 + 1 - core)

    def source(t):
        dx, dz = ORDER[t]
        p2, z2 = chip(dx, 4 - dz)
        return p2 * 4 + z2

    def unit_of(j):
        unit = 20 * z + 2 * j + core
        head, block = lax.div(unit, 16), lax.rem(unit, 16)
        return head, block

    for j in range(UNITS):
        head, block = unit_of(j)

        @pl.when(block != col)
        def _():
            remote(qpack.at[0], qbuf.at[j], q_s.at[0], q_r.at[j], (row, block)).wait_recv()

    @pl.loop(0, UNITS)
    def _(j):
        packed = qbuf[pl.ds(j, 1)].reshape(128, LANES).astype(F32)
        low = jnp.where(half, packed, 0.0).astype(BF16)
        high = jnp.where(half, swap(packed), 0.0).astype(BF16)
        queries[pl.ds(pl.multiple_of(256 * j, 256), 256)] = jnp.concatenate([low, high], axis=0)

    lane = lax.broadcasted_iota(jnp.int32, (1, LANES), 1)
    keep = jnp.where(lane < 64, 0.0, 1.0).astype(BF16)
    ones = jnp.where(lane < 64, 1.0, 0.0).astype(BF16)
    for number, blocks in enumerate(STAGES):
        start, end = number == 0, number == len(STAGES) - 1
        width = 256 * len(blocks)
        slots = []
        for kind, t in blocks:
            g = source(t)
            if kind == "own":
                if t:
                    remote(
                        kv.at[pl.ds(0, 2)], kvbuf.at[core, g], kv_s.at[t], kv_r.at[t], sibling
                    ).wait_recv()
                send(remote(kvbuf.at[core, g], kvbuf.at[core, g], fw_s.at[t], fw_r.at[t], sibling))
                slots.append((core, g))
        for kind, t in blocks:
            g = source(t)
            if kind == "sib":
                remote(
                    kvbuf.at[core, g], kvbuf.at[1 - core, g], fw_s.at[t], fw_r.at[t], sibling
                ).wait_recv()
                slots.append((1 - core, g))
        for head in range(2):
            for i, (parity, g) in enumerate(slots):
                block = kvbuf[pl.ds(parity, 1), pl.ds(g, 1), head].reshape(256, LANES)
                vstage[0, head, 256 * i : 256 * i + 256, :] = block
                vstage[1, head, 256 * i : 256 * i + 256, :] = block * keep + ones

        for pair in range(UNITS // 2):
            rows = slice(512 * pair, 512 * pair + 512)
            slot = unit_of(2 * pair)[0] - z
            k = vstage[0, pl.ds(slot, 1), 0:width].reshape(width, LANES)
            v = vstage[1, pl.ds(slot, 1), 0:width].reshape(width, LANES)
            scores = lax.dot_general(
                queries[rows], k, (((1,), (1,)), ((), ())), preferred_element_type=F32
            )
            most = jnp.broadcast_to(jnp.max(scores, axis=1, keepdims=True), (512, LANES))
            if not start:
                before = highest[rows]
                most = jnp.maximum(most, before)
            expo = jnp.exp(scores - jnp.concatenate([most] * (width // LANES), axis=1))
            total = dot(expo.astype(BF16), v)
            if not start:
                total += accum[rows] * jnp.exp(before - most)
            if not end:
                highest[rows] = most
                accum[rows] = total
                continue
            total = total / swap(total)
            for i in range(2):
                j = 2 * pair + i
                a, b = total[256 * i : 256 * i + 128], total[256 * i + 128 : 256 * i + 256]
                opack[j] = jnp.where(half, swap(a), b).astype(BF16)
                head, block = unit_of(j)
                whole = 5 * plane + head
                send(remote(opack.at[j], back.at[whole], o_s.at[j], o_r.at[whole], (row, block)), block != col)

                @pl.when(block == col)
                def _():
                    back[pl.ds(whole, 1)] = opack[j][None]

    for head in range(10):
        frm, slot = place_of(head)

        @pl.when(frm != col)
        def _():
            remote(opack.at[0], back.at[head], o_s.at[0], o_r.at[head], (row, frm)).wait_recv()

    tiles = []
    for i in range(5):
        a, b = back[2 * i].astype(F32), back[2 * i + 1].astype(F32)
        tiles.append(
            jnp.concatenate([jnp.where(half, a, swap(b)), jnp.where(half, swap(a), b)], axis=0)
        )
    attended = jnp.concatenate(tiles, axis=1).astype(BF16)
    mixed = (inner[...].astype(F32) + dot(attended, wd[4]) + out_b[...].reshape(1, C)).astype(BF16)
    result[...] = (resnet[...].astype(F32) + dot(mixed, wd[5]) + proj_b[...].reshape(1, C)).astype(BF16)

    for leave in leaving:
        leave()

def shards(
    latent, gn1_gain, gn1_bias, conv1_weight, conv1_bias, time_shift, gn2_gain, gn2_bias,
    conv2_weight, conv2_bias, gn3_gain, gn3_bias, in_weight, in_bias, ln_gain, ln_bias,
    query_weight, key_weight, value_weight, out_weight, out_bias, proj_weight, proj_bias,
):
    lat = latent.transpose(0, 2, 1, 3).reshape(8, 32, C)
    hbm = pl.BlockSpec(memory_space=pl.ANY)
    vmem = pl.BlockSpec(memory_space=pltpu.VMEM)
    dma = pltpu.SemaphoreType.DMA
    result = pl.pallas_call(
        kernel,
        out_shape=jax.ShapeDtypeStruct((OWN * ROWS, C), BF16),
        in_specs=[vmem] + [hbm] * 8 + [vmem] * 14,
        out_specs=vmem,
        scratch_shapes=[
            pltpu.VMEM((3, 3 * C, C), BF16),
            pltpu.VMEM((3, 3 * C, C), BF16),
            pltpu.VMEM((6, C, C), BF16),
            pltpu.VMEM((C, C), BF16),
            pltpu.VMEM((8, 32, C), BF16),
            pltpu.VMEM((8, ROWS, C), BF16),
            pltpu.VMEM((3, 16, 2, C), F32),
            pltpu.VMEM((8, C), F32),
            pltpu.VMEM((8, ROWS, 3 * C), BF16),
            pltpu.VMEM((6 * ROWS, C), F32),
            pltpu.VMEM((256, C), BF16),
            pltpu.VMEM((256, C), BF16),
            pltpu.VMEM((10, 128, LANES), BF16),
            pltpu.VMEM((10, 256, LANES), BF16),
            pltpu.VMEM((UNITS, 128, LANES), BF16),
            pltpu.VMEM((UNITS * 256, LANES), BF16),
            pltpu.VMEM((2, 8, 2, 256, LANES), BF16),
            pltpu.VMEM((2, 2, 1024, LANES), BF16),
            pltpu.VMEM((UNITS * 256, LANES), F32),
            pltpu.VMEM((UNITS * 256, LANES), F32),
            pltpu.VMEM((UNITS, 128, LANES), BF16),
            pltpu.VMEM((10, 128, LANES), BF16),
            dma((24,)), dma((8,)), dma((8,)), dma((2,)), dma((2,)), dma((3, 16)), dma((3, 16)),
            dma((10,)), dma((10,)), dma((8,)), dma((8,)), dma((8,)), dma((8,)),
            dma((10,)), dma((10,)),
        ],
        compiler_params=pltpu.CompilerParams(
            collective_id=0, has_side_effects=True, vmem_limit_bytes=56 * 2**20
        ),
        cost_estimate=pl.CostEstimate(
            flops=8 * 10**9, bytes_accessed=21 * 10**6, transcendentals=11 * 10**6
        ),
    )(
        lat, conv1_weight, conv2_weight, in_weight, query_weight, key_weight, value_weight,
        out_weight, proj_weight, gn1_gain, gn1_bias, conv1_bias, time_shift,
        gn2_gain, gn2_bias, conv2_bias, gn3_gain, gn3_bias,
        in_bias, ln_gain, ln_bias, out_bias, proj_bias,
    )
    return result.reshape(OWN, ROWS, C).transpose(1, 0, 2)[None]


def solution(mesh):
    placed = (P(None, "row", "col", None),) + (P(),) * 22
    return jax.shard_map(
        shards, mesh=mesh, in_specs=placed, out_specs=P("row", None, "col", None), check_vma=False
    )
```

```python
import jax
import jax.numpy as jnp
from jax import lax
from jax.experimental import pallas as pl
from jax.experimental.pallas import tpu as pltpu
from jax.sharding import PartitionSpec as P

MESH = pl.DeviceIdType.MESH
F32 = jnp.float32
BF16 = jnp.bfloat16
C = 640
ROWS = 64
OWN = 4
CELLS = 64 * 64 * 20
LANES = 128
UNITS = 10
ORDER = [(0, 0), (1, 0), (0, 1), (0, 3), (1, 1), (1, 3), (0, 2), (1, 2)]
STAGES = [
    [(kind, t) for kind in ("own", "sib") for t in chunks]
    for chunks in ((0,), (1, 2, 3), (4, 5), (6, 7))
]


def dot(a, b):
    return jnp.dot(a, b, preferred_element_type=F32)


def kernel(
    lat, conv1_w, conv2_w, in_w, q_w, k_w, v_w, out_w, proj_w,
    gn1_g, gn1_b, conv1_b, tshift, gn2_g, gn2_b, conv2_b, gn3_g, gn3_b,
    in_b, ln_g, ln_b, out_b, proj_b,
    result,
    w1, w2, wd, group, xin, cells, xcol, edge, stats, parts, taps, conv, resnet, inner,
    qpack, kv, qbuf, queries, kvbuf, vstage, accum, highest, opack, back,
    wsem, a2a_s, a2a_r, halo_s, halo_r, st_s, st_r, q_s, q_r, kv_s, kv_r, fw_s, fw_r, o_s, o_r,
):
    row = lax.axis_index("row")
    col = lax.axis_index("col")
    plane, z, core = lax.div(col, 8), lax.rem(lax.div(col, 2), 4), lax.rem(col, 2)

    def remote(src, dst, send, recv, where):
        return pltpu.make_async_remote_copy(
            src_ref=src, dst_ref=dst, send_sem=send, recv_sem=recv,
            device_id=where, device_id_type=MESH,
        )

    leaving = []

    def send(copy, when=None):
        def start():
            copy.start()

        def leave():
            copy.wait_send()

        if when is None:
            start()
            leaving.append(leave)
        else:
            pl.when(when)(start)
            leaving.append(lambda: pl.when(when)(leave))

    loads = []

    def load(src, dst):
        copy = pltpu.make_async_copy(src, dst, wsem.at[next(used)])
        copy.start()
        loads.append(copy)

    def loaded(count):
        for copy in loads[:count]:
            copy.wait()
        del loads[:count]

    used = iter(range(24))

    def load_conv(source, target):
        for dx in range(3):
            for dy in range(3):
                load(source.at[dy, dx], target.at[dx, pl.ds(dy * C, C)])

    load_conv(conv1_w, w1)

    barrier = pltpu.get_barrier_semaphore()
    for t in range(1, 8):
        pl.semaphore_signal(
            barrier, inc=1, device_id=(lax.rem(row + t, 8), col), device_id_type=MESH
        )
    for t in range(1, 16):
        pl.semaphore_signal(
            barrier, inc=1, device_id=(row, lax.rem(col + t, 16)), device_id_type=MESH
        )
    one = lax.shift_right_logical(lax.broadcasted_iota(jnp.int32, (C, C), 0) * 52429, 20)
    two = lax.shift_right_logical(lax.broadcasted_iota(jnp.int32, (C, C), 1) * 52429, 20)
    group[...] = jnp.where(one == two, 1.0, 0.0).astype(BF16)
    parts[...] = jnp.zeros_like(parts)
    xin[pl.ds(row, 1)] = lat[pl.ds(row, 1)]
    pl.semaphore_wait(barrier, 22)

    for t in range(1, 8):
        to = lax.rem(row + t, 8)
        send(remote(lat.at[to], xin.at[row], a2a_s.at[t], a2a_r.at[t], (to, col)))
    arrived = [
        remote(lat.at[0], xin.at[lax.rem(row + 8 - t, 8)], a2a_s.at[t], a2a_r.at[t], (lax.rem(row + t, 8), col))
        for t in range(1, 8)
    ]
    for copy in arrived:
        copy.wait_recv()
    load_conv(conv2_w, w2)
    for i, source in enumerate((in_w, q_w, k_w, v_w, out_w, proj_w)):
        load(source, wd.at[i])
    first = jnp.zeros((8, C), F32)
    second = jnp.zeros((8, C), F32)
    for i in range(8):
        for j in range(8):
            cell = xin[i, j].astype(F32)
            for k in range(5):
                cells[k, 32 * i + 4 * j : 32 * i + 4 * j + 4, :] = cell[:, k * LANES : (k + 1) * LANES]
    for j in range(OWN):
        column = jnp.concatenate(
            [cells[k, pl.ds(j, ROWS, stride=OWN), :] for k in range(5)], axis=1
        )
        xcol[1 + j] = column.astype(BF16)
        column = column.reshape(8, 8, C)
        first = first + jnp.sum(column, axis=0)
        second = second + jnp.sum(column * column, axis=0)

    right, left = lax.rem(col + 1, 16), lax.rem(col + 15, 16)
    halos = [
        remote(xcol.at[4], xcol.at[0], halo_s.at[0], halo_r.at[0], (row, right)),
        remote(xcol.at[1], xcol.at[5], halo_s.at[1], halo_r.at[1], (row, left)),
    ]
    borders = [
        remote(edge.at[1], edge.at[2], halo_s.at[2], halo_r.at[2], (row, right)),
        remote(edge.at[0], edge.at[3], halo_s.at[3], halo_r.at[3], (row, left)),
    ]
    def send_sums(phase, first, second):
        stats[phase, pl.ds(col, 1)] = jnp.concatenate(
            [jnp.sum(first, axis=0, keepdims=True), jnp.sum(second, axis=0, keepdims=True)], axis=0
        )[None]
        for t in range(1, 16):
            send(remote(
                stats.at[phase, col], stats.at[phase, col], st_s.at[phase, t], st_r.at[phase, t],
                (row, lax.rem(col + t, 16)),
            ))

    def take_sums(phase, gain, bias, epsilon):
        for t in range(1, 16):
            remote(
                stats.at[phase, col], stats.at[phase, lax.rem(col + 16 - t, 16)],
                st_s.at[phase, t], st_r.at[phase, t], (row, lax.rem(col + t, 16)),
            ).wait_recv()
        total = jnp.sum(stats[phase], axis=0)
        high = total.astype(BF16).astype(F32)
        rest = total - high
        middle = rest.astype(BF16).astype(F32)
        parts[0:2] = high
        parts[2:4] = middle
        parts[4:6] = rest - middle
        spread = dot(parts[...].astype(BF16), group[...])
        mean = (spread[0:1] + spread[2:3] + spread[4:5]) * (1.0 / CELLS)
        square = (spread[1:2] + spread[3:4] + spread[5:6]) * (1.0 / CELLS)
        scale = lax.rsqrt(square - mean * mean + epsilon) * gain[...].reshape(1, C)
        return scale, bias[...].reshape(1, C) - mean * scale

    def put_taps(place, values, scale, shift, column):
        v = values * scale + shift
        act = 0.5 * v * (1.0 + jnp.tanh(0.5 * v))
        act = jnp.where((column >= 0) & (column < 64), act, 0.0)
        index = lax.broadcasted_iota(jnp.int32, (ROWS, C), 0)
        above = jnp.where(index == 0, 0.0, pltpu.roll(act, 1, 0))
        below = jnp.where(index == ROWS - 1, 0.0, pltpu.roll(act, ROWS - 1, 0))
        taps[pl.ds(place, 1), :, 0:C] = above.astype(BF16)[None]
        taps[pl.ds(place, 1), :, C : 2 * C] = act.astype(BF16)[None]
        taps[pl.ds(place, 1), :, 2 * C : 3 * C] = below.astype(BF16)[None]

    for copy in halos:
        send(copy)
    send_sums(0, first, second)
    scale1, shift1 = take_sums(0, gn1_g, gn1_b, 1e-5)
    for copy in halos:
        copy.wait_recv()

    @pl.loop(0, 6)
    def _(j):
        values = xcol[pl.ds(j, 1)].reshape(ROWS, C).astype(F32)
        put_taps(j, values, scale1, shift1, 4 * col - 1 + j)

    loaded(9)
    conv[...] = jnp.broadcast_to(conv1_b[...].reshape(1, C) + tshift[pl.ds(row, 1), :], conv.shape)

    @pl.loop(0, 3)
    def _(dx):
        lhs = taps[pl.ds(dx, 4)].reshape(4 * ROWS, 3 * C)
        conv[...] += dot(lhs, w1[pl.ds(dx, 1)].reshape(3 * C, C))

    edge[0] = conv[0:ROWS, :].astype(BF16)
    edge[1] = conv[3 * ROWS : 4 * ROWS, :].astype(BF16)
    for copy in borders:
        send(copy)
    own = conv[...].reshape(32, 8, C)
    send_sums(1, jnp.sum(own, axis=0), jnp.sum(own * own, axis=0))
    scale2, shift2 = take_sums(1, gn2_g, gn2_b, 1e-5)

    @pl.loop(0, 4)
    def _(j):
        values = conv[pl.ds(pl.multiple_of(j * ROWS, ROWS), ROWS), :]
        put_taps(j + 1, values, scale2, shift2, 4 * col + j)

    for copy in borders:
        copy.wait_recv()

    @pl.loop(0, 2)
    def _(j):
        values = edge[pl.ds(2 + j, 1)].reshape(ROWS, C).astype(F32)
        put_taps(5 * j, values, scale2, shift2, 4 * col - 1 + 5 * j)

    loaded(9)
    conv[...] = xcol[1:5].reshape(4 * ROWS, C).astype(F32) + conv2_b[...].reshape(1, C)

    @pl.loop(0, 3)
    def _(dx):
        lhs = taps[pl.ds(dx, 4)].reshape(4 * ROWS, 3 * C)
        conv[...] += dot(lhs, w2[pl.ds(dx, 1)].reshape(3 * C, C))

    resnet[...] = conv[...].astype(BF16)
    rounded = resnet[...].astype(F32).reshape(32, 8, C)
    send_sums(2, jnp.sum(rounded, axis=0), jnp.sum(rounded * rounded, axis=0))
    loaded(6)
    scale3, shift3 = take_sums(2, gn3_g, gn3_b, 1e-6)

    attn_in = (resnet[...].astype(F32) * scale3 + shift3).astype(BF16)
    inner[...] = (dot(attn_in, wd[0]) + in_b[...].reshape(1, C)).astype(BF16)
    v = inner[...].astype(F32)
    centered = v - jnp.mean(v, axis=-1, keepdims=True)
    variance = jnp.mean(centered * centered, axis=-1, keepdims=True)
    normed = (centered * lax.rsqrt(variance + 1e-5) * ln_g[...].reshape(1, C) + ln_b[...].reshape(1, C)).astype(BF16)

    half = lax.broadcasted_iota(jnp.int32, (128, LANES), 1) < 64
    half2 = lax.broadcasted_iota(jnp.int32, (256, LANES), 1) < 64

    def swap(a):
        return pltpu.roll(a, 64, 1)

    keys = dot(normed, wd[2])
    values = dot(normed, wd[3])
    for i in range(5):
        a, b = keys[:, i * LANES : (i + 1) * LANES], values[:, i * LANES : (i + 1) * LANES]
        kv[2 * i] = jnp.where(half2, a, swap(b)).astype(BF16)
        kv[2 * i + 1] = jnp.where(half2, swap(a), b).astype(BF16)

    def chip(dx, dz):
        return lax.rem(plane + dx, 2), lax.rem(z + dz, 4)

    here = plane * 4 + z
    kvbuf[pl.ds(core, 1), pl.ds(here, 1)] = kv[pl.ds(5 * plane + z, 2)][None, None]

    def send_keys(number):
        for kind, t in STAGES[number]:
            if kind == "sib" or t == 0:
                continue
            p2, z2 = chip(*ORDER[t])
            send(remote(
                kv.at[pl.ds(5 * p2 + z2, 2)], kvbuf.at[core, here], kv_s.at[t], kv_r.at[t],
                (row, p2 * 8 + z2 * 2 + core),
            ))

    send_keys(1)

    q = dot(normed, wd[1]).astype(BF16).astype(F32) * 0.125
    for i in range(5):
        a, b = q[0:128, i * LANES : (i + 1) * LANES], q[128:256, i * LANES : (i + 1) * LANES]
        qpack[2 * i] = jnp.where(half, a, swap(b)).astype(BF16)
        qpack[2 * i + 1] = jnp.where(half, swap(a), b).astype(BF16)

    def place_of(head):
        unit = 16 * (head % 5) + col
        return (head // 5) * 8 + lax.div(unit, 20) * 2 + core, lax.div(lax.rem(unit, 20), 2)

    for head in range(10):
        to, slot = place_of(head)
        send(remote(qpack.at[head], qbuf.at[slot], q_s.at[head], q_r.at[slot], (row, to)), to != col)

        @pl.when(to == col)
        def _():
            qbuf[pl.ds(slot, 1)] = qpack[head][None]

    sibling = (row, plane * 8 + z * 2 + 1 - core)

    def source(t):
        dx, dz = ORDER[t]
        p2, z2 = chip(dx, 4 - dz)
        return p2 * 4 + z2

    def unit_of(j):
        unit = 20 * z + 2 * j + core
        head, block = lax.div(unit, 16), lax.rem(unit, 16)
        return head, block

    def take_queries():
        for j in range(UNITS):
            head, block = unit_of(j)

            @pl.when(block != col)
            def _():
                remote(qpack.at[0], qbuf.at[j], q_s.at[0], q_r.at[j], (row, block)).wait_recv()

        send_keys(2)
        @pl.loop(0, UNITS)
        def _(j):
            packed = qbuf[pl.ds(j, 1)].reshape(128, LANES).astype(F32)
            low = jnp.where(half, packed, 0.0).astype(BF16)
            high = jnp.where(half, swap(packed), 0.0).astype(BF16)
            queries[pl.ds(pl.multiple_of(256 * j, 256), 256)] = jnp.concatenate([low, high], axis=0)

    lane = lax.broadcasted_iota(jnp.int32, (1, LANES), 1)
    keep = jnp.where(lane < 64, 0.0, 1.0).astype(BF16)
    ones = jnp.where(lane < 64, 1.0, 0.0).astype(BF16)
    for number, blocks in enumerate(STAGES):
        start, end = number == 0, number == len(STAGES) - 1
        width = 256 * len(blocks)
        slots = []
        for kind, t in blocks:
            g = source(t)
            if kind == "own":
                if t:
                    remote(
                        kv.at[pl.ds(0, 2)], kvbuf.at[core, g], kv_s.at[t], kv_r.at[t], sibling
                    ).wait_recv()
                send(remote(kvbuf.at[core, g], kvbuf.at[core, g], fw_s.at[t], fw_r.at[t], sibling))
                slots.append((core, g))
        if number == 1:
            send_keys(3)
        for kind, t in blocks:
            g = source(t)
            if kind == "sib":
                remote(
                    kvbuf.at[core, g], kvbuf.at[1 - core, g], fw_s.at[t], fw_r.at[t], sibling
                ).wait_recv()
                slots.append((1 - core, g))
        for head in range(2):
            for i, (parity, g) in enumerate(slots):
                block = kvbuf[pl.ds(parity, 1), pl.ds(g, 1), head].reshape(256, LANES)
                vstage[0, head, 256 * i : 256 * i + 256, :] = block
                vstage[1, head, 256 * i : 256 * i + 256, :] = block * keep + ones

        if start:
            take_queries()
        for pair in range(UNITS // 2):
            rows = slice(512 * pair, 512 * pair + 512)
            slot = unit_of(2 * pair)[0] - z
            k = vstage[0, pl.ds(slot, 1), 0:width].reshape(width, LANES)
            v = vstage[1, pl.ds(slot, 1), 0:width].reshape(width, LANES)
            scores = lax.dot_general(
                queries[rows], k, (((1,), (1,)), ((), ())), preferred_element_type=F32
            )
            most = jnp.broadcast_to(jnp.max(scores, axis=1, keepdims=True), (512, LANES))
            if not start:
                before = highest[rows]
                most = jnp.maximum(most, before)
            expo = jnp.exp(scores - jnp.concatenate([most] * (width // LANES), axis=1))
            total = dot(expo.astype(BF16), v)
            if not start:
                total += accum[rows] * jnp.exp(before - most)
            if not end:
                highest[rows] = most
                accum[rows] = total
                continue
            total = total / swap(total)
            for i in range(2):
                j = 2 * pair + i
                a, b = total[256 * i : 256 * i + 128], total[256 * i + 128 : 256 * i + 256]
                opack[j] = jnp.where(half, swap(a), b).astype(BF16)
                head, block = unit_of(j)
                whole = 5 * plane + head
                send(remote(opack.at[j], back.at[whole], o_s.at[j], o_r.at[whole], (row, block)), block != col)

                @pl.when(block == col)
                def _():
                    back[pl.ds(whole, 1)] = opack[j][None]

    for head in range(10):
        frm, slot = place_of(head)

        @pl.when(frm != col)
        def _():
            remote(opack.at[0], back.at[head], o_s.at[0], o_r.at[head], (row, frm)).wait_recv()

    tiles = []
    for i in range(5):
        a, b = back[2 * i].astype(F32), back[2 * i + 1].astype(F32)
        tiles.append(
            jnp.concatenate([jnp.where(half, a, swap(b)), jnp.where(half, swap(a), b)], axis=0)
        )
    attended = jnp.concatenate(tiles, axis=1).astype(BF16)
    mixed = (inner[...].astype(F32) + dot(attended, wd[4]) + out_b[...].reshape(1, C)).astype(BF16)
    result[...] = (resnet[...].astype(F32) + dot(mixed, wd[5]) + proj_b[...].reshape(1, C)).astype(BF16)

    for leave in leaving:
        leave()

def shards(
    latent, gn1_gain, gn1_bias, conv1_weight, conv1_bias, time_shift, gn2_gain, gn2_bias,
    conv2_weight, conv2_bias, gn3_gain, gn3_bias, in_weight, in_bias, ln_gain, ln_bias,
    query_weight, key_weight, value_weight, out_weight, out_bias, proj_weight, proj_bias,
):
    hbm = pl.BlockSpec(memory_space=pl.ANY)
    vmem = pl.BlockSpec(memory_space=pltpu.VMEM)
    dma = pltpu.SemaphoreType.DMA
    result = pl.pallas_call(
        kernel,
        out_shape=jax.ShapeDtypeStruct((OWN * ROWS, C), BF16),
        in_specs=[vmem] + [hbm] * 8 + [vmem] * 14,
        out_specs=vmem,
        scratch_shapes=[
            pltpu.VMEM((3, 3 * C, C), BF16),
            pltpu.VMEM((3, 3 * C, C), BF16),
            pltpu.VMEM((6, C, C), BF16),
            pltpu.VMEM((C, C), BF16),
            pltpu.VMEM((8, 8, OWN, C), BF16),
            pltpu.VMEM((5, OWN * ROWS, LANES), F32),
            pltpu.VMEM((6, ROWS, C), BF16),
            pltpu.VMEM((4, ROWS, C), BF16),
            pltpu.VMEM((3, 16, 2, C), F32),
            pltpu.VMEM((8, C), F32),
            pltpu.VMEM((6, ROWS, 3 * C), BF16),
            pltpu.VMEM((OWN * ROWS, C), F32),
            pltpu.VMEM((256, C), BF16),
            pltpu.VMEM((256, C), BF16),
            pltpu.VMEM((10, 128, LANES), BF16),
            pltpu.VMEM((10, 256, LANES), BF16),
            pltpu.VMEM((UNITS, 128, LANES), BF16),
            pltpu.VMEM((UNITS * 256, LANES), BF16),
            pltpu.VMEM((2, 8, 2, 256, LANES), BF16),
            pltpu.VMEM((2, 2, 1536, LANES), BF16),
            pltpu.VMEM((UNITS * 256, LANES), F32),
            pltpu.VMEM((UNITS * 256, LANES), F32),
            pltpu.VMEM((UNITS, 128, LANES), BF16),
            pltpu.VMEM((10, 128, LANES), BF16),
            dma((24,)), dma((8,)), dma((8,)), dma((4,)), dma((4,)), dma((3, 16)), dma((3, 16)),
            dma((10,)), dma((10,)), dma((8,)), dma((8,)), dma((8,)), dma((8,)),
            dma((10,)), dma((10,)),
        ],
        compiler_params=pltpu.CompilerParams(
            collective_id=0, has_side_effects=True, vmem_limit_bytes=56 * 2**20
        ),
        cost_estimate=pl.CostEstimate(
            flops=8 * 10**9, bytes_accessed=21 * 10**6, transcendentals=11 * 10**6
        ),
    )(
        latent, conv1_weight, conv2_weight, in_weight, query_weight, key_weight, value_weight,
        out_weight, proj_weight, gn1_gain, gn1_bias, conv1_bias, time_shift,
        gn2_gain, gn2_bias, conv2_bias, gn3_gain, gn3_bias,
        in_bias, ln_gain, ln_bias, out_bias, proj_bias,
    )
    return result.reshape(OWN, ROWS, C).transpose(1, 0, 2)[None]


def solution(mesh):
    placed = (P(None, "row", "col", None),) + (P(),) * 22
    return jax.shard_map(
        shards, mesh=mesh, in_specs=placed, out_specs=P("row", None, "col", None), check_vma=False
    )
```

```python
import jax
import jax.numpy as jnp
from jax import lax
from jax.experimental import pallas as pl
from jax.experimental.pallas import tpu as pltpu
from jax.sharding import PartitionSpec as P

MESH = pl.DeviceIdType.MESH
F32 = jnp.float32
BF16 = jnp.bfloat16
C = 640
ROWS = 64
OWN = 4
CELLS = 64 * 64 * 20
LANES = 128
UNITS = 10
ORDER = [(0, 0), (1, 0), (0, 1), (0, 3), (1, 1), (1, 3), (0, 2), (1, 2)]
STAGES = [
    [(kind, t) for kind in ("own", "sib") for t in chunks]
    for chunks in ((0,), (1, 2, 3), (4, 5, 6), (7,))
]


def dot(a, b):
    return jnp.dot(a, b, preferred_element_type=F32)


def kernel(
    lat, conv1_w, conv2_w, in_w, q_w, k_w, v_w, out_w, proj_w,
    gn1_g, gn1_b, conv1_b, tshift, gn2_g, gn2_b, conv2_b, gn3_g, gn3_b,
    in_b, ln_g, ln_b, out_b, proj_b,
    result,
    w1, w2, wd, group, xin, cells, xcol, edge, stats, parts, taps, conv, resnet, inner,
    qpack, kv, qbuf, queries, kvbuf, vstage, accum, highest, opack, back,
    wsem, a2a_s, a2a_r, halo_s, halo_r, st_s, st_r, q_s, q_r, kv_s, kv_r, fw_s, fw_r, o_s, o_r,
):
    row = lax.axis_index("row")
    col = lax.axis_index("col")
    plane, z, core = lax.div(col, 8), lax.rem(lax.div(col, 2), 4), lax.rem(col, 2)

    def remote(src, dst, send, recv, where):
        return pltpu.make_async_remote_copy(
            src_ref=src, dst_ref=dst, send_sem=send, recv_sem=recv,
            device_id=where, device_id_type=MESH,
        )

    leaving = []

    def send(copy, when=None):
        def start():
            copy.start()

        def leave():
            copy.wait_send()

        if when is None:
            start()
            leaving.append(leave)
        else:
            pl.when(when)(start)
            leaving.append(lambda: pl.when(when)(leave))

    loads = []

    def load(src, dst):
        copy = pltpu.make_async_copy(src, dst, wsem.at[next(used)])
        copy.start()
        loads.append(copy)

    def loaded(count):
        for copy in loads[:count]:
            copy.wait()
        del loads[:count]

    used = iter(range(24))

    def load_conv(source, target):
        for dx in range(3):
            for dy in range(3):
                load(source.at[dy, dx], target.at[dx, pl.ds(dy * C, C)])

    barrier = pltpu.get_barrier_semaphore()
    for t in range(1, 8):
        pl.semaphore_signal(
            barrier, inc=1, device_id=(lax.rem(row + t, 8), col), device_id_type=MESH
        )
    for t in range(1, 16):
        pl.semaphore_signal(
            barrier, inc=1, device_id=(row, lax.rem(col + t, 16)), device_id_type=MESH
        )
    pl.semaphore_wait(barrier, 22)

    for t in range(1, 8):
        to = lax.rem(row + t, 8)
        send(remote(lat.at[to], xin.at[row], a2a_s.at[t], a2a_r.at[t], (to, col)))
    load_conv(conv1_w, w1)
    one = lax.shift_right_logical(lax.broadcasted_iota(jnp.int32, (C, C), 0) * 52429, 20)
    two = lax.shift_right_logical(lax.broadcasted_iota(jnp.int32, (C, C), 1) * 52429, 20)
    group[...] = jnp.where(one == two, 1.0, 0.0).astype(BF16)
    parts[...] = jnp.zeros_like(parts)
    xin[pl.ds(row, 1)] = lat[pl.ds(row, 1)]
    arrived = [
        remote(lat.at[0], xin.at[lax.rem(row + 8 - t, 8)], a2a_s.at[t], a2a_r.at[t], (lax.rem(row + t, 8), col))
        for t in range(1, 8)
    ]
    for copy in arrived:
        copy.wait_recv()
    load_conv(conv2_w, w2)
    for i, source in enumerate((in_w, q_w, k_w, v_w, out_w, proj_w)):
        load(source, wd.at[i])
    first = jnp.zeros((8, C), F32)
    second = jnp.zeros((8, C), F32)
    for i in range(8):
        for j in range(8):
            cell = xin[i, j].astype(F32)
            for k in range(5):
                cells[k, 32 * i + 4 * j : 32 * i + 4 * j + 4, :] = cell[:, k * LANES : (k + 1) * LANES]
    for j in range(OWN):
        column = jnp.concatenate(
            [cells[k, pl.ds(j, ROWS, stride=OWN), :] for k in range(5)], axis=1
        )
        xcol[1 + j] = column.astype(BF16)
        column = column.reshape(8, 8, C)
        first = first + jnp.sum(column, axis=0)
        second = second + jnp.sum(column * column, axis=0)

    right, left = lax.rem(col + 1, 16), lax.rem(col + 15, 16)
    halos = [
        remote(xcol.at[4], xcol.at[0], halo_s.at[0], halo_r.at[0], (row, right)),
        remote(xcol.at[1], xcol.at[5], halo_s.at[1], halo_r.at[1], (row, left)),
    ]
    borders = [
        remote(edge.at[1], edge.at[2], halo_s.at[2], halo_r.at[2], (row, right)),
        remote(edge.at[0], edge.at[3], halo_s.at[3], halo_r.at[3], (row, left)),
    ]
    def send_sums(phase, first, second):
        stats[phase, pl.ds(col, 1)] = jnp.concatenate(
            [jnp.sum(first, axis=0, keepdims=True), jnp.sum(second, axis=0, keepdims=True)], axis=0
        )[None]
        for t in range(1, 16):
            send(remote(
                stats.at[phase, col], stats.at[phase, col], st_s.at[phase, t], st_r.at[phase, t],
                (row, lax.rem(col + t, 16)),
            ))

    def take_sums(phase, gain, bias, epsilon):
        for t in range(1, 16):
            remote(
                stats.at[phase, col], stats.at[phase, lax.rem(col + 16 - t, 16)],
                st_s.at[phase, t], st_r.at[phase, t], (row, lax.rem(col + t, 16)),
            ).wait_recv()
        total = jnp.sum(stats[phase], axis=0)
        high = total.astype(BF16).astype(F32)
        rest = total - high
        middle = rest.astype(BF16).astype(F32)
        parts[0:2] = high
        parts[2:4] = middle
        parts[4:6] = rest - middle
        spread = dot(parts[...].astype(BF16), group[...])
        mean = (spread[0:1] + spread[2:3] + spread[4:5]) * (1.0 / CELLS)
        square = (spread[1:2] + spread[3:4] + spread[5:6]) * (1.0 / CELLS)
        scale = lax.rsqrt(square - mean * mean + epsilon) * gain[...].reshape(1, C)
        return scale, bias[...].reshape(1, C) - mean * scale

    def put_taps(place, values, scale, shift, column):
        v = values * scale + shift
        act = 0.5 * v * (1.0 + jnp.tanh(0.5 * v))
        act = jnp.where((column >= 0) & (column < 64), act, 0.0)
        index = lax.broadcasted_iota(jnp.int32, (ROWS, C), 0)
        above = jnp.where(index == 0, 0.0, pltpu.roll(act, 1, 0))
        below = jnp.where(index == ROWS - 1, 0.0, pltpu.roll(act, ROWS - 1, 0))
        taps[pl.ds(place, 1), :, 0:C] = above.astype(BF16)[None]
        taps[pl.ds(place, 1), :, C : 2 * C] = act.astype(BF16)[None]
        taps[pl.ds(place, 1), :, 2 * C : 3 * C] = below.astype(BF16)[None]

    for copy in halos:
        send(copy)
    send_sums(0, first, second)
    scale1, shift1 = take_sums(0, gn1_g, gn1_b, 1e-5)
    for copy in halos:
        copy.wait_recv()

    @pl.loop(0, 6)
    def _(j):
        values = xcol[pl.ds(j, 1)].reshape(ROWS, C).astype(F32)
        put_taps(j, values, scale1, shift1, 4 * col - 1 + j)

    loaded(9)
    conv[...] = jnp.broadcast_to(conv1_b[...].reshape(1, C) + tshift[pl.ds(row, 1), :], conv.shape)

    @pl.loop(0, 3)
    def _(dx):
        lhs = taps[pl.ds(dx, 4)].reshape(4 * ROWS, 3 * C)
        conv[...] += dot(lhs, w1[pl.ds(dx, 1)].reshape(3 * C, C))

    edge[0] = conv[0:ROWS, :].astype(BF16)
    edge[1] = conv[3 * ROWS : 4 * ROWS, :].astype(BF16)
    for copy in borders:
        send(copy)
    own = conv[...].reshape(32, 8, C)
    send_sums(1, jnp.sum(own, axis=0), jnp.sum(own * own, axis=0))
    scale2, shift2 = take_sums(1, gn2_g, gn2_b, 1e-5)

    @pl.loop(0, 4)
    def _(j):
        values = conv[pl.ds(pl.multiple_of(j * ROWS, ROWS), ROWS), :]
        put_taps(j + 1, values, scale2, shift2, 4 * col + j)

    for copy in borders:
        copy.wait_recv()

    @pl.loop(0, 2)
    def _(j):
        values = edge[pl.ds(2 + j, 1)].reshape(ROWS, C).astype(F32)
        put_taps(5 * j, values, scale2, shift2, 4 * col - 1 + 5 * j)

    loaded(9)
    conv[...] = xcol[1:5].reshape(4 * ROWS, C).astype(F32) + conv2_b[...].reshape(1, C)

    @pl.loop(0, 3)
    def _(dx):
        lhs = taps[pl.ds(dx, 4)].reshape(4 * ROWS, 3 * C)
        conv[...] += dot(lhs, w2[pl.ds(dx, 1)].reshape(3 * C, C))

    resnet[...] = conv[...].astype(BF16)
    rounded = resnet[...].astype(F32).reshape(32, 8, C)
    send_sums(2, jnp.sum(rounded, axis=0), jnp.sum(rounded * rounded, axis=0))
    loaded(6)
    scale3, shift3 = take_sums(2, gn3_g, gn3_b, 1e-6)

    attn_in = (resnet[...].astype(F32) * scale3 + shift3).astype(BF16)
    inner[...] = (dot(attn_in, wd[0]) + in_b[...].reshape(1, C)).astype(BF16)
    v = inner[...].astype(F32)
    centered = v - jnp.mean(v, axis=-1, keepdims=True)
    variance = jnp.mean(centered * centered, axis=-1, keepdims=True)
    normed = (centered * lax.rsqrt(variance + 1e-5) * ln_g[...].reshape(1, C) + ln_b[...].reshape(1, C)).astype(BF16)

    half = lax.broadcasted_iota(jnp.int32, (128, LANES), 1) < 64
    half2 = lax.broadcasted_iota(jnp.int32, (256, LANES), 1) < 64

    def swap(a):
        return pltpu.roll(a, 64, 1)

    q = dot(normed, wd[1]).astype(BF16).astype(F32) * 0.125
    for i in range(5):
        a, b = q[0:128, i * LANES : (i + 1) * LANES], q[128:256, i * LANES : (i + 1) * LANES]
        qpack[2 * i] = jnp.where(half, a, swap(b)).astype(BF16)
        qpack[2 * i + 1] = jnp.where(half, swap(a), b).astype(BF16)

    def place_of(head):
        unit = 16 * (head % 5) + col
        return (head // 5) * 8 + lax.div(unit, 20) * 2 + core, lax.div(lax.rem(unit, 20), 2)

    for head in range(10):
        to, slot = place_of(head)
        send(remote(qpack.at[head], qbuf.at[slot], q_s.at[head], q_r.at[slot], (row, to)), to != col)

        @pl.when(to == col)
        def _():
            qbuf[pl.ds(slot, 1)] = qpack[head][None]

    keys = dot(normed, wd[2])
    values = dot(normed, wd[3])
    for i in range(5):
        a, b = keys[:, i * LANES : (i + 1) * LANES], values[:, i * LANES : (i + 1) * LANES]
        kv[2 * i] = jnp.where(half2, a, swap(b)).astype(BF16)
        kv[2 * i + 1] = jnp.where(half2, swap(a), b).astype(BF16)

    def chip(dx, dz):
        return lax.rem(plane + dx, 2), lax.rem(z + dz, 4)

    here = plane * 4 + z
    kvbuf[pl.ds(core, 1), pl.ds(here, 1)] = kv[pl.ds(5 * plane + z, 2)][None, None]

    def send_keys(number):
        for kind, t in STAGES[number]:
            if kind == "sib" or t == 0:
                continue
            p2, z2 = chip(*ORDER[t])
            send(remote(
                kv.at[pl.ds(5 * p2 + z2, 2)], kvbuf.at[core, here], kv_s.at[t], kv_r.at[t],
                (row, p2 * 8 + z2 * 2 + core),
            ))

    send_keys(1)

    sibling = (row, plane * 8 + z * 2 + 1 - core)

    def source(t):
        dx, dz = ORDER[t]
        p2, z2 = chip(dx, 4 - dz)
        return p2 * 4 + z2

    def unit_of(j):
        unit = 20 * z + 2 * j + core
        head, block = lax.div(unit, 16), lax.rem(unit, 16)
        return head, block

    def take_queries():
        for j in range(UNITS):
            head, block = unit_of(j)

            @pl.when(block != col)
            def _():
                remote(qpack.at[0], qbuf.at[j], q_s.at[0], q_r.at[j], (row, block)).wait_recv()

        send_keys(2)
        @pl.loop(0, UNITS)
        def _(j):
            packed = qbuf[pl.ds(j, 1)].reshape(128, LANES).astype(F32)
            low = jnp.where(half, packed, 0.0).astype(BF16)
            high = jnp.where(half, swap(packed), 0.0).astype(BF16)
            queries[pl.ds(pl.multiple_of(256 * j, 256), 256)] = jnp.concatenate([low, high], axis=0)

    lane = lax.broadcasted_iota(jnp.int32, (1, LANES), 1)
    keep = jnp.where(lane < 64, 0.0, 1.0).astype(BF16)
    ones = jnp.where(lane < 64, 1.0, 0.0).astype(BF16)
    for number, blocks in enumerate(STAGES):
        start, end = number == 0, number == len(STAGES) - 1
        width = 256 * len(blocks)
        slots = []
        for kind, t in blocks:
            g = source(t)
            if kind == "own":
                if t:
                    remote(
                        kv.at[pl.ds(0, 2)], kvbuf.at[core, g], kv_s.at[t], kv_r.at[t], sibling
                    ).wait_recv()
                send(remote(kvbuf.at[core, g], kvbuf.at[core, g], fw_s.at[t], fw_r.at[t], sibling))
                slots.append((core, g))
        if number == 1:
            send_keys(3)
        for kind, t in blocks:
            g = source(t)
            if kind == "sib":
                remote(
                    kvbuf.at[core, g], kvbuf.at[1 - core, g], fw_s.at[t], fw_r.at[t], sibling
                ).wait_recv()
                slots.append((1 - core, g))
        for head in range(2):
            for i, (parity, g) in enumerate(slots):
                block = kvbuf[pl.ds(parity, 1), pl.ds(g, 1), head].reshape(256, LANES)
                vstage[head, 256 * i : 256 * i + 256, :] = block * keep + ones

        if start:
            take_queries()
        for pair in range(UNITS // 2):
            rows = slice(512 * pair, 512 * pair + 512)
            slot = unit_of(2 * pair)[0] - z
            k = jnp.concatenate(
                [
                    kvbuf[pl.ds(parity, 1), pl.ds(g, 1), pl.ds(slot, 1)].reshape(256, LANES)
                    for parity, g in slots
                ],
                axis=0,
            )
            v = vstage[pl.ds(slot, 1), 0:width].reshape(width, LANES)
            scores = lax.dot_general(
                queries[rows], k, (((1,), (1,)), ((), ())), preferred_element_type=F32
            )
            most = jnp.broadcast_to(jnp.max(scores, axis=1, keepdims=True), (512, LANES))
            if not start:
                before = highest[rows]
                most = jnp.maximum(most, before)
            expo = jnp.exp(scores - jnp.concatenate([most] * (width // LANES), axis=1))
            total = dot(expo.astype(BF16), v)
            if not start:
                total += accum[rows] * jnp.exp(before - most)
            if not end:
                highest[rows] = most
                accum[rows] = total
                continue
            total = total / swap(total)
            for i in range(2):
                j = 2 * pair + i
                a, b = total[256 * i : 256 * i + 128], total[256 * i + 128 : 256 * i + 256]
                opack[j] = jnp.where(half, swap(a), b).astype(BF16)
                head, block = unit_of(j)
                whole = 5 * plane + head
                send(remote(opack.at[j], back.at[whole], o_s.at[j], o_r.at[whole], (row, block)), block != col)

                @pl.when(block == col)
                def _():
                    back[pl.ds(whole, 1)] = opack[j][None]

    for head in range(10):
        frm, slot = place_of(head)

        @pl.when(frm != col)
        def _():
            remote(opack.at[0], back.at[head], o_s.at[0], o_r.at[head], (row, frm)).wait_recv()

    tiles = []
    for i in range(5):
        a, b = back[2 * i].astype(F32), back[2 * i + 1].astype(F32)
        tiles.append(
            jnp.concatenate([jnp.where(half, a, swap(b)), jnp.where(half, swap(a), b)], axis=0)
        )
    attended = jnp.concatenate(tiles, axis=1).astype(BF16)
    mixed = (inner[...].astype(F32) + dot(attended, wd[4]) + out_b[...].reshape(1, C)).astype(BF16)
    result[...] = (resnet[...].astype(F32) + dot(mixed, wd[5]) + proj_b[...].reshape(1, C)).astype(BF16)

    for leave in leaving:
        leave()

def shards(
    latent, gn1_gain, gn1_bias, conv1_weight, conv1_bias, time_shift, gn2_gain, gn2_bias,
    conv2_weight, conv2_bias, gn3_gain, gn3_bias, in_weight, in_bias, ln_gain, ln_bias,
    query_weight, key_weight, value_weight, out_weight, out_bias, proj_weight, proj_bias,
):
    hbm = pl.BlockSpec(memory_space=pl.ANY)
    vmem = pl.BlockSpec(memory_space=pltpu.VMEM)
    dma = pltpu.SemaphoreType.DMA
    result = pl.pallas_call(
        kernel,
        out_shape=jax.ShapeDtypeStruct((OWN * ROWS, C), BF16),
        in_specs=[vmem] + [hbm] * 8 + [vmem] * 14,
        out_specs=vmem,
        scratch_shapes=[
            pltpu.VMEM((3, 3 * C, C), BF16),
            pltpu.VMEM((3, 3 * C, C), BF16),
            pltpu.VMEM((6, C, C), BF16),
            pltpu.VMEM((C, C), BF16),
            pltpu.VMEM((8, 8, OWN, C), BF16),
            pltpu.VMEM((5, OWN * ROWS, LANES), F32),
            pltpu.VMEM((6, ROWS, C), BF16),
            pltpu.VMEM((4, ROWS, C), BF16),
            pltpu.VMEM((3, 16, 2, C), F32),
            pltpu.VMEM((8, C), F32),
            pltpu.VMEM((6, ROWS, 3 * C), BF16),
            pltpu.VMEM((OWN * ROWS, C), F32),
            pltpu.VMEM((256, C), BF16),
            pltpu.VMEM((256, C), BF16),
            pltpu.VMEM((10, 128, LANES), BF16),
            pltpu.VMEM((10, 256, LANES), BF16),
            pltpu.VMEM((UNITS, 128, LANES), BF16),
            pltpu.VMEM((UNITS * 256, LANES), BF16),
            pltpu.VMEM((2, 8, 2, 256, LANES), BF16),
            pltpu.VMEM((2, 1536, LANES), BF16),
            pltpu.VMEM((UNITS * 256, LANES), F32),
            pltpu.VMEM((UNITS * 256, LANES), F32),
            pltpu.VMEM((UNITS, 128, LANES), BF16),
            pltpu.VMEM((10, 128, LANES), BF16),
            dma((24,)), dma((8,)), dma((8,)), dma((4,)), dma((4,)), dma((3, 16)), dma((3, 16)),
            dma((10,)), dma((10,)), dma((8,)), dma((8,)), dma((8,)), dma((8,)),
            dma((10,)), dma((10,)),
        ],
        compiler_params=pltpu.CompilerParams(
            collective_id=0, has_side_effects=True, vmem_limit_bytes=56 * 2**20
        ),
        cost_estimate=pl.CostEstimate(
            flops=8 * 10**9, bytes_accessed=21 * 10**6, transcendentals=11 * 10**6
        ),
    )(
        latent, conv1_weight, conv2_weight, in_weight, query_weight, key_weight, value_weight,
        out_weight, proj_weight, gn1_gain, gn1_bias, conv1_bias, time_shift,
        gn2_gain, gn2_bias, conv2_bias, gn3_gain, gn3_bias,
        in_bias, ln_gain, ln_bias, out_bias, proj_bias,
    )
    return result.reshape(OWN, ROWS, C).transpose(1, 0, 2)[None]


def solution(mesh):
    placed = (P(None, "row", "col", None),) + (P(),) * 22
    return jax.shard_map(
        shards, mesh=mesh, in_specs=placed, out_specs=P("row", None, "col", None), check_vma=False
    )
```
